512 devices in a mesh: item: 32 (over y, z_hi, core), code: 16 (over z_lo, x).
Axes of the slice: x: 4, y: 4, z: 16 (z_hi: 4, z_lo: 4; z = z_hi * 4 + z_lo), core: 2. Of those that a mesh axis runs over, the one named last changes fastest.
Arguments:
- embeddings: bfloat16 [512, 262144], P('code', 'item'), may hold values from -6 to 6
- first_codes: int32 [262144], P('item'), may hold values from 0 to 8191
- second_codes: int32 [262144], P('item'), may hold values from 0 to 8191
- first_old: float32 [512, 8192], P('code', 'item'), may hold values from -6 to 6
- second_old: float32 [512, 8192], P('code', 'item'), may hold values from -3 to 3
Outputs:
- first_new: float32 [512, 8192], P('code', 'item')
- second_new: float32 [512, 8192], P('code', 'item')
- leftover: float32 [512, 262144], P('code', 'item')
The draws below stay inside these ranges and needn't reach their ends.
All inputs are finite; a program needn't handle non-finite values.
Results may differ from the reference program's by a relative error of at most 0.0003.
Values sent between devices are 32-bit elements; how exact they have to be, the bound alone decides.
No kernel may reach another device: no remote copies, remote signals or barrier semaphores. Data moves between devices by JAX's collectives and lax.ppermute only.
A program may use at most 64 MiB of HBM per device.

```python
import jax
import jax.numpy as jnp
from jax import lax

D = 512
K = 8192
ITEMS = 262144


def plant(values, rng, low, largest):
    index_at = [jax.random.randint(jax.random.fold_in(rng, axis), (), 0, length) for axis, length in enumerate(values.shape)]
    widest = values.shape.index(max(values.shape))
    neighbour = index_at[:widest] + [(index_at[widest] + 1) % values.shape[widest]] + index_at[widest + 1:]
    return values.at[tuple(index_at)].set(low).at[tuple(neighbour)].set(largest)


def levels(rng, shape, cuts, low, high):
    level, own = 1.0, jax.random.fold_in(rng, 6)
    for axis_at, blocks in cuts:
        draws = jnp.exp(jax.random.uniform(jax.random.fold_in(own, axis_at), (blocks,), jnp.float32, low / len(cuts), high / len(cuts)))
        level = level * jnp.repeat(draws, shape[axis_at] // blocks).reshape([-1 if axis == axis_at else 1 for axis in range(len(shape))])
    return level


def bell_draw(rng, extent, deviation, reach, split=(), held_as=jnp.bfloat16):
    values = deviation * jax.random.normal(rng, extent, jnp.float32)
    if split:
        values = values * levels(rng, extent, split, -0.22, 0.18)
    return jnp.clip(values, -reach, reach).astype(held_as)


def setup_inputs(seed: int = 0) -> dict:
    arg_keys = jax.random.split(jax.random.key(seed), 6)
    embeddings = bell_draw(arg_keys[0], (D, ITEMS), 1.0, 6.0, ((0, 16), (1, 32)))
    first_codes = plant(jax.random.randint(arg_keys[1], (ITEMS,), 0, K), jax.random.fold_in(arg_keys[1], 1), 0, K - 1).astype(jnp.int32)
    second_codes = plant(jax.random.randint(arg_keys[2], (ITEMS,), 0, K), jax.random.fold_in(arg_keys[2], 1), 0, K - 1).astype(jnp.int32)
    first_old = bell_draw(arg_keys[3], (D, K), 1.0, 6.0, ((0, 16), (1, 32)), jnp.float32)
    second_old = bell_draw(arg_keys[4], (D, K), 0.5, 3.0, ((0, 16), (1, 32)), jnp.float32)
    return {"embeddings": embeddings, "first_codes": first_codes, "second_codes": second_codes, "first_old": first_old, "second_old": second_old}


def update(columns, codes, old):
    sums = jax.ops.segment_sum(columns.T, codes, num_segments=K).T
    counts = jax.ops.segment_sum(jnp.ones(codes.shape, jnp.float32), codes, num_segments=K)
    return 0.5 * old + 0.5 * sums / (counts + 1.0)[None, :]

def reference(embeddings, first_codes, second_codes, first_old, second_old):
    values = embeddings.astype(jnp.float32)
    normed = values * jax.lax.rsqrt(lax.optimization_barrier(jnp.mean(values * values, axis=0, keepdims=True)) + 1e-06)
    first_new = update(normed, first_codes, first_old)
    middle = normed - jnp.take(first_new, first_codes, axis=1)
    second_new = update(middle, second_codes, second_old)
    leftover = middle - jnp.take(second_new, second_codes, axis=1)
    return (first_new, second_new, leftover)
```

```python
import functools

import jax
import jax.numpy as jnp
from jax import lax
from jax.experimental import pallas as pl
from jax.experimental.pallas import tpu as pltpu
from jax.sharding import Mesh
from jax.sharding import PartitionSpec as P

D = 512
HI = 32
LO = 256
Y = 4
Z = 4
F = 16
PER = HI // Y
BLOCK = PER * F + PER
TILE = 2048
BF = jnp.bfloat16
F32 = jnp.float32
NT = (((1,), (1,)), ((), ()))


def split(v):
    top = v.astype(BF)
    return top, (v - top.astype(F32)).astype(BF)


def hi_lo(code):
    code = code.astype(jnp.int32)
    return (code >> 8).astype(F32).astype(BF), (code & (LO - 1)).astype(F32).astype(BF)


def rows_of(count, columns):
    return lax.broadcasted_iota(jnp.int32, (count, columns), 0).astype(F32).astype(BF)


def ones_where(mask):
    return jnp.where(mask, jnp.ones((), BF), jnp.zeros((), BF))


def one_hot(lo):
    return ones_where(lo == rows_of(LO, lo.shape[1]))


def masked(v, hi):
    zero = jnp.zeros((), BF)
    return [jnp.where(hi == jnp.array(h, BF), v, zero) for h in range(HI)]


def add_sums(values, code, init_ref, out_ref):
    hi, lo = hi_lo(code)
    top, rest = split(values)
    members = ones_where(hi == rows_of(HI, hi.shape[1]))
    left = jnp.concatenate(masked(top, hi) + masked(rest, hi) + [members], axis=0)
    s = lax.dot_general(left, one_hot(lo), NT, preferred_element_type=F32)
    half = HI * F
    sums = s[:half] + s[half : 2 * half]
    counts = s[2 * half :]

    @pl.when(pl.program_id(0) == 0)
    def _():
        out_ref[...] = jnp.zeros_like(out_ref) if init_ref is None else init_ref[...]

    for y in range(Y):
        out_ref[y, : PER * F, :] += sums[y * PER * F : (y + 1) * PER * F]
        out_ref[y, PER * F :, :] += counts[y * PER : (y + 1) * PER]


def looked_up(code, table_ref):
    hi, lo = hi_lo(code)
    hot = one_hot(lo)
    top, rest = split(table_ref[...])
    g = jnp.dot(top, hot, preferred_element_type=F32) + jnp.dot(rest, hot, preferred_element_type=F32)
    hi = hi.astype(F32)
    found = g[:F]
    for h in range(1, HI):
        found = jnp.where(hi == h, g[h * F : (h + 1) * F], found)
    return found


def first_kernel(with_init, values_ref, codes_ref, *refs):
    init_ref = refs[0] if with_init else None
    add_sums(values_ref[...], codes_ref[0:1], init_ref, refs[-1])


def second_kernel(with_init, values_ref, codes_ref, table_ref, *refs):
    init_ref = refs[0] if with_init else None
    middle_ref, out_ref = refs[-2:]
    middle = values_ref[...] - looked_up(codes_ref[0:1], table_ref)
    middle_ref[...] = middle
    add_sums(middle, codes_ref[1:2], init_ref, out_ref)


def last_kernel(middle_ref, codes_ref, table_ref, out_ref):
    out_ref[...] = middle_ref[...] - looked_up(codes_ref[1:2], table_ref)


def per_tile(rows, at=0):
    return pl.BlockSpec((rows, TILE), lambda i: (at, i))


def whole(*shape):
    return pl.BlockSpec(shape, lambda i: (0,) * len(shape))


SUMS = jax.ShapeDtypeStruct((Y, BLOCK, LO), F32)
PARAMS = pltpu.CompilerParams(vmem_limit_bytes=56 << 20)


def first_sums(packed, init=None):
    n = packed.shape[1]
    extra = [] if init is None else [init]
    return pl.pallas_call(
        functools.partial(first_kernel, init is not None),
        grid=(n // TILE,),
        in_specs=[per_tile(F), per_tile(8, F // 8)] + [whole(Y, BLOCK, LO)] * len(extra),
        out_specs=whole(Y, BLOCK, LO),
        out_shape=SUMS,
        compiler_params=PARAMS,
        name="first_sums",
    )(packed, packed, *extra)


def second_sums(packed, table, init=None):
    n = packed.shape[1]
    extra = [] if init is None else [init]
    return pl.pallas_call(
        functools.partial(second_kernel, init is not None),
        grid=(n // TILE,),
        in_specs=[per_tile(F), per_tile(8, F // 8), whole(HI * F, LO)] + [whole(Y, BLOCK, LO)] * len(extra),
        out_specs=(per_tile(F), whole(Y, BLOCK, LO)),
        out_shape=(jax.ShapeDtypeStruct((F, n), F32), SUMS),
        compiler_params=PARAMS,
        name="second_sums",
    )(packed, packed, table, *extra)


def last_lookup(middle, packed, table):
    n = middle.shape[1]
    return pl.pallas_call(
        last_kernel,
        grid=(n // TILE,),
        in_specs=[per_tile(F), per_tile(8, F // 8), whole(HI * F, LO)],
        out_specs=per_tile(F),
        out_shape=jax.ShapeDtypeStruct((F, n), F32),
        compiler_params=PARAMS,
        name="last_lookup",
    )(middle, packed, table)


def to_all(v, axis):
    return lax.all_to_all(jnp.broadcast_to(v[None], (4, *v.shape)), axis, 0, 0, tiled=True)


def swap_core(v):
    return lax.ppermute(v, "core", [(0, 1), (1, 0)])


def z_partners(first):
    steps = (1, 3) if first else (3, 1)
    return [(2 * z + c, 2 * (z ^ steps[c]) + c) for z in range(Z) for c in range(2)]


def updated(sums, old, core, zh):
    z_core = ("zh", "core")
    own = lax.all_to_all(sums, "y", 0, 0, tiled=True).sum(axis=0)
    olds = old.reshape(2 * F, LO)
    got = lax.ppermute(jnp.concatenate([own, olds]), z_core, z_partners(True))
    own = own + got[:BLOCK]
    olds = jnp.concatenate([olds, got[BLOCK:]])
    got = lax.ppermute(jnp.concatenate([own, olds]), z_core, z_partners(False))
    own = own + got[:BLOCK]
    olds = jnp.concatenate([olds, got[BLOCK:]]).reshape(Z, 2, F, LO)
    place = jnp.where(core == 0, jnp.array([0, 1, 3, 2]), jnp.array([0, 2, 3, 1]))
    olds = jnp.concatenate([lax.dynamic_slice_in_dim(olds, place[z ^ zh], 1) for z in range(Z)]).reshape(PER, F, LO)
    counts = own[PER * F :]
    new = 0.5 * olds + 0.5 * own[: PER * F].reshape(PER, F, LO) / (counts + 1.0)[:, None]
    return new, to_all(new, "y").reshape(HI * F, LO)


def on_device(e, first_codes, second_codes, first_old, second_old):
    core, zh = lax.axis_index("core"), lax.axis_index("zh")
    n = e.shape[1]
    values = e.astype(F32)
    squares = jnp.sum(values * values, axis=0)
    squares = to_all(squares, "x").sum(axis=0)
    squares = to_all(squares, "zl").sum(axis=0)
    normed = values * lax.rsqrt(squares / D + 1e-06)[None, :]
    codes = jnp.stack([first_codes, second_codes]).astype(F32)

    def packed(half):
        part = functools.partial(lax.dynamic_slice_in_dim, start_index=half * F, slice_size=F)
        olds = jnp.concatenate([part(first_old), part(second_old)]).reshape(1, n)
        return jnp.concatenate([part(normed), codes, olds, jnp.zeros((5, n), F32)])

    mine = packed(core)
    theirs = swap_core(packed(1 - core))

    def old_of(level):
        a, b = (v[F + 2].reshape(2, F, LO)[level] for v in (mine, theirs))
        return jnp.where(core == 0, jnp.stack([a, b]), jnp.stack([b, a]))

    sums = first_sums(theirs, first_sums(mine))
    first_block, first_table = updated(sums, old_of(0), core, zh)
    my_middle, sums = second_sums(mine, first_table)
    their_middle, sums = second_sums(theirs, first_table, sums)
    second_block, second_table = updated(sums, old_of(1), core, zh)
    their_rest = last_lookup(their_middle, theirs, second_table)

    def owned(block, at):
        return lax.dynamic_index_in_dim(block, 2 * zh + at, keepdims=False)

    tail = jnp.concatenate([owned(first_block, 1 - core), owned(second_block, 1 - core)]).reshape(1, n)
    got = swap_core(jnp.concatenate([their_rest, tail]))
    my_rest = last_lookup(my_middle, mine, second_table)
    got_new = got[F].reshape(2, F, LO)

    def joined(a, b):
        return jnp.where(core == 0, jnp.concatenate([a, b]), jnp.concatenate([b, a]))

    first_new = joined(owned(first_block, core), got_new[0])
    second_new = joined(owned(second_block, core), got_new[1])
    return first_new, second_new, joined(my_rest, got[:F])


def solution(mesh):
    grid = Mesh(mesh.devices.reshape(Y, Z, 2, 4, 4), ("y", "zh", "core", "zl", "x"))
    item, code = ("y", "zh", "core"), ("zl", "x")
    both = P(code, item)
    return jax.shard_map(
        on_device,
        mesh=grid,
        in_specs=(both, P(item), P(item), both, both),
        out_specs=(both, both, both),
        check_vma=False,
    )
```

```python
import functools

import jax
import jax.numpy as jnp
from jax import lax
from jax.experimental import pallas as pl
from jax.experimental.pallas import tpu as pltpu
from jax.sharding import Mesh
from jax.sharding import PartitionSpec as P

D = 512
HI = 16
LO = 512
Y = 4
Z = 4
F = 16
SUM_ROWS = Z * F
BLOCK = SUM_ROWS + 8
TILE = 4096
CHUNK = 1024
BF = jnp.bfloat16
F32 = jnp.float32
NT = (((1,), (1,)), ((), ()))
PARTS = 1
WIDTH = LO // PARTS


def split(v):
    top = v.astype(BF)
    return top, (v - top.astype(F32)).astype(BF)


def hi_lo(code):
    code = code.astype(jnp.int32)
    return (code >> 9).astype(F32).astype(BF), (code & (LO - 1)).astype(F32)


def rows_of(count, columns):
    return lax.broadcasted_iota(jnp.int32, (count, columns), 0).astype(F32)


def ones_where(mask):
    return jnp.where(mask, jnp.ones((), BF), jnp.zeros((), BF))


def one_hot(lo):
    upper = jnp.where(lo >= 256, 1.0, 0.0)
    lower = (lo - 256 * upper).astype(BF)
    upper = upper.astype(BF)
    rows = rows_of(256, lo.shape[1]).astype(BF)
    none = jnp.array(-1, BF)
    return jnp.concatenate(
        [ones_where(jnp.where(upper == jnp.array(u, BF), lower, none) == rows) for u in range(2)], axis=0
    )


def masked(v, hi):
    zero = jnp.zeros((), BF)
    return [jnp.where(hi == jnp.array(h, BF), v, zero) for h in range(HI)]


def add_sums(values, hi, hot, out_refs):
    top, rest = split(values)
    members = ones_where(hi == rows_of(HI, hi.shape[1]).astype(BF))
    left = jnp.concatenate(masked(top, hi) + masked(rest, hi) + [members], axis=0)
    s = lax.dot_general(left, hot, NT, preferred_element_type=F32)
    half = HI * F
    sums = s[:half] + s[half : 2 * half]
    counts = s[2 * half :]
    for p, out_ref in enumerate(out_refs):
        columns = slice(p * WIDTH, (p + 1) * WIDTH)
        for y in range(Y):
            out_ref[y, :SUM_ROWS, :] += sums[y * SUM_ROWS : (y + 1) * SUM_ROWS, columns]
            out_ref[y, SUM_ROWS : SUM_ROWS + Z, :] += counts[y * Z : (y + 1) * Z, columns]


def looked_up(terms, hi, hot):
    g = jnp.dot(terms, jnp.concatenate([hot, hot], axis=0), preferred_element_type=F32)
    hi = hi.astype(F32)
    found = g[:F]
    for h in range(1, HI):
        found = jnp.where(hi == h, g[h * F : (h + 1) * F], found)
    return found


def terms_of(table_refs):
    tops, rests = zip(*(split(ref[...]) for ref in table_refs), strict=True)
    return jnp.concatenate([*tops, *rests], axis=1)


def chunks(body):
    for at in range(0, TILE, CHUNK):
        body(slice(at, at + CHUNK))


def squares_kernel(e_ref, out_ref):
    values = e_ref[...].astype(F32)
    total = jnp.sum(values * values, axis=0, keepdims=True)
    for at in range(out_ref.shape[0]):
        out_ref[at] = total


def first_kernel(with_init, values_ref, codes_ref, *refs):
    out_refs = refs[-PARTS:]

    @pl.when(pl.program_id(0) == 0)
    def _():
        for p, out_ref in enumerate(out_refs):
            out_ref[...] = refs[p][...] if with_init else jnp.zeros_like(out_ref)

    def body(at):
        hi, lo = hi_lo(codes_ref[0:1, at])
        add_sums(values_ref[:, at], hi, one_hot(lo), out_refs)

    chunks(body)


def second_kernel(tiles, mine_ref, my_codes_ref, theirs_ref, their_codes_ref, *refs):
    table_refs, middle_ref, out_refs = refs[:PARTS], refs[PARTS], refs[PARTS + 1 :]
    step = pl.program_id(0)
    terms = terms_of(table_refs)

    @pl.when(step == 0)
    def _():
        for out_ref in out_refs:
            out_ref[...] = jnp.zeros_like(out_ref)

    def body(at):
        values = jnp.where(step < tiles, mine_ref[:, at], theirs_ref[:, at])
        codes = jnp.where(step < tiles, my_codes_ref[0:2, at], their_codes_ref[0:2, at])
        hi, lo = hi_lo(codes[0:1])
        middle = values - looked_up(terms, hi, one_hot(lo))
        middle_ref[:, at] = middle
        hi, lo = hi_lo(codes[1:2])
        add_sums(middle, hi, one_hot(lo), out_refs)

    chunks(body)


def last_kernel(middle_ref, codes_ref, *refs):
    table_refs, out_ref = refs[:PARTS], refs[PARTS]
    terms = terms_of(table_refs)

    def body(at):
        hi, lo = hi_lo(codes_ref[1:2, at])
        out_ref[:, at] = middle_ref[:, at] - looked_up(terms, hi, one_hot(lo))

    chunks(body)


def whole(*shape):
    return pl.BlockSpec(shape, lambda *i: (0,) * len(shape))


def cost(products, columns):
    return pl.CostEstimate(flops=products * 4 * HI * F * LO * columns, bytes_accessed=8 * F * columns, transcendentals=0)


SUMS = [jax.ShapeDtypeStruct((Y, BLOCK, WIDTH), F32)] * PARTS
SUM_SPECS = [whole(Y, BLOCK, WIDTH)] * PARTS
TABLE_SPECS = [whole(HI * F, WIDTH)] * PARTS
PARAMS = pltpu.CompilerParams(vmem_limit_bytes=28 << 20)


def squares_of(e, copies):
    rows, n = e.shape
    return pl.pallas_call(
        squares_kernel,
        grid=(2,),
        in_specs=[pl.BlockSpec((rows, n // 2), lambda i: (0, i))],
        out_specs=pl.BlockSpec((copies, 1, n // 2), lambda i: (0, 0, i)),
        out_shape=jax.ShapeDtypeStruct((copies, 1, n), F32),
        compiler_params=PARAMS,
        name="squares",
    )(e)


def first_sums(packed, init=()):
    n = packed.shape[1]
    return pl.pallas_call(
        functools.partial(first_kernel, len(init) > 0),
        grid=(n // TILE,),
        in_specs=[pl.BlockSpec((F, TILE), lambda i: (0, i)), pl.BlockSpec((8, TILE), lambda i: (F // 8, i))]
        + SUM_SPECS[: len(init)],
        out_specs=SUM_SPECS,
        out_shape=SUMS,
        compiler_params=PARAMS,
        cost_estimate=cost(1, n),
        name="first_sums",
    )(packed, packed, *init)


def second_sums(mine, theirs, tables):
    n = mine.shape[1]
    tiles = n // TILE

    def early(i):
        return jnp.minimum(i, tiles - 1)

    def late(i):
        return jnp.maximum(i - tiles, 0)

    return pl.pallas_call(
        functools.partial(second_kernel, tiles),
        grid=(2 * tiles,),
        in_specs=[
            pl.BlockSpec((F, TILE), lambda i: (0, early(i))),
            pl.BlockSpec((8, TILE), lambda i: (F // 8, early(i))),
            pl.BlockSpec((F, TILE), lambda i: (0, late(i))),
            pl.BlockSpec((8, TILE), lambda i: (F // 8, late(i))),
            *TABLE_SPECS,
        ],
        out_specs=[pl.BlockSpec((F, TILE), lambda i: (0, i)), *SUM_SPECS],
        out_shape=[jax.ShapeDtypeStruct((F, 2 * n), F32), *SUMS],
        compiler_params=PARAMS,
        cost_estimate=cost(2, 2 * n),
        name="second_sums",
    )(mine, mine, theirs, theirs, *tables)


def last_lookup(middle, part, packed, tables):
    n = packed.shape[1]
    tiles = n // TILE
    return pl.pallas_call(
        last_kernel,
        grid=(tiles,),
        in_specs=[
            pl.BlockSpec((F, TILE), lambda i: (0, part * tiles + i)),
            pl.BlockSpec((8, TILE), lambda i: (F // 8, i)),
            *TABLE_SPECS,
        ],
        out_specs=pl.BlockSpec((F, TILE), lambda i: (0, i)),
        out_shape=jax.ShapeDtypeStruct((F, n), F32),
        compiler_params=PARAMS,
        cost_estimate=cost(1, n),
        name="last_lookup",
    )(middle, packed, *tables)


def to_all(v, axis, size=4):
    return lax.all_to_all(jnp.broadcast_to(v[None], (size, *v.shape)), axis, 0, 0, tiled=True)


def swap_core(v):
    return lax.ppermute(v, "core", [(0, 1), (1, 0)])


def swap_z(v, first):
    steps = (1, 3) if first else (3, 1)
    pairs = [(2 * z + c, 2 * (z ^ steps[c]) + c) for z in range(Z) for c in range(2)]
    return lax.ppermute(v, ("zh", "core"), pairs)


def at_y(parts):
    return [lax.all_to_all(part, "y", 0, 0, tiled=True).sum(axis=0) for part in parts]


def over_z(parts, first):
    return [part + swap_z(part, first) for part in parts]


def over_z_with(parts, old, core, zh):
    (own,) = parts
    got = swap_z(jnp.concatenate([own, old]), True)
    own, olds = own + got[:BLOCK], [old, got[BLOCK:]]
    got = swap_z(jnp.concatenate([own, *olds]), False)
    own, olds = own + got[:BLOCK], jnp.stack([*olds, got[BLOCK : BLOCK + F], got[BLOCK + F :]])
    near, far = jnp.where(core == 0, olds[1], olds[2]), jnp.where(core == 0, olds[2], olds[1])
    olds = jnp.stack([olds[0], near, olds[3], far])
    olds = jnp.where(zh % 2 == 0, olds, jnp.stack([olds[1], olds[0], olds[3], olds[2]]))
    olds = jnp.where(zh < 2, olds, jnp.concatenate([olds[2:], olds[:2]]))
    return [own], olds


def updated(parts, olds):
    news = []
    for p, own in enumerate(parts):
        counts = own[SUM_ROWS : SUM_ROWS + Z, None, :]
        old = olds[:, :, p * WIDTH : (p + 1) * WIDTH]
        news.append(0.5 * old + 0.5 * own[:SUM_ROWS].reshape(Z, F, WIDTH) / (counts + 1.0))
    return news


def tables_of(news):
    return [to_all(new, "y").reshape(HI * F, WIDTH) for new in news]


def on_device(e, first_codes, second_codes, first_old, second_old):
    core, zh = lax.axis_index("core"), lax.axis_index("zh")
    n = e.shape[1]

    def feature_half(v, which, axis):
        return lax.dynamic_slice_in_dim(v, which * F, F, axis)

    def by_core(mine, theirs, axis):
        return jnp.where(core == 0, jnp.concatenate([mine, theirs], axis), jnp.concatenate([theirs, mine], axis))

    def whole_columns(news):
        own = lax.dynamic_index_in_dim(jnp.concatenate(news, axis=2), zh, keepdims=False)
        first, last = own[:, :256], own[:, 256:]
        kept, sent = jnp.where(core == 0, first, last), jnp.where(core == 0, last, first)
        return kept, swap_core(sent)

    values = e.astype(F32)
    squares = lax.all_to_all(squares_of(e, 4), "x", 0, 0, tiled=True).reshape(4, n).sum(axis=0)
    squares = to_all(squares, "zl").sum(axis=0)
    normed = values * lax.rsqrt(squares / D + 1e-06)[None, :]
    codes = jnp.stack([first_codes, second_codes]).astype(F32)

    def packed(half):
        olds = jnp.stack([feature_half(first_old, half, 0), feature_half(second_old, half, 0)])
        return jnp.concatenate([feature_half(normed, half, 0), codes, olds.reshape(1, n), jnp.zeros((5, n), F32)])

    mine = packed(core)
    theirs = swap_core(packed(1 - core))

    sums = first_sums(theirs, first_sums(mine))
    olds = by_core(mine[F + 2].reshape(2, F, 256), theirs[F + 2].reshape(2, F, 256), 2)
    own, first_all = over_z_with(at_y(sums), olds[0], core, zh)
    first_news = updated(own, first_all)
    middle, *sums = second_sums(mine, theirs, tables_of(first_news))
    own = at_y(sums)
    own, first_news = lax.optimization_barrier((own, first_news))
    own, second_all = over_z_with(own, olds[1], core, zh)
    first_columns = whole_columns(first_news)
    own, first_new = lax.optimization_barrier((own, by_core(*first_columns, 0)))
    second_news = updated(own, second_all)
    second_columns = whole_columns(second_news)
    tables, second_new = lax.optimization_barrier((tables_of(second_news), by_core(*second_columns, 0)))
    their_rest = last_lookup(middle, 1, theirs, tables)
    got = swap_core(their_rest)
    my_rest = last_lookup(middle, 0, mine, tables)
    return first_new, second_new, by_core(my_rest, got, 0)


def solution(mesh):
    grid = Mesh(mesh.devices.reshape(Y, Z, 2, 4, 4), ("y", "zh", "core", "zl", "x"))
    item, code = ("y", "zh", "core"), ("zl", "x")
    both = P(code, item)
    return jax.shard_map(
        on_device,
        mesh=grid,
        in_specs=(both, P(item), P(item), both, both),
        out_specs=(both, both, both),
        check_vma=False,
    )
```

```python
import functools

import jax
import jax.numpy as jnp
from jax import lax
from jax.experimental import pallas as pl
from jax.experimental.pallas import tpu as pltpu
from jax.sharding import Mesh
from jax.sharding import PartitionSpec as P

D = 512
HI = 16
LO = 512
Y = 4
Z = 4
F = 16
SUM_ROWS = Z * F
BLOCK = SUM_ROWS + 8
TILE = 4096
CHUNK = 4096
BF = jnp.bfloat16
F8 = jnp.float8_e4m3fn
REST_MAX = 256.0
F32 = jnp.float32
NT = (((1,), (1,)), ((), ()))
PARTS = 1
WIDTH = LO // PARTS


def split(v):
    top = v.astype(BF)
    largest = jnp.maximum(jnp.max(jnp.abs(v), keepdims=True), 1e-30)
    scale = (REST_MAX * 256.0) / largest
    return top, (v - top.astype(F32)) * scale, largest * (1.0 / (REST_MAX * 256.0))


def hi_lo(code):
    code = code.astype(jnp.int32)
    return (code >> 9).astype(F32).astype(BF), (code & (LO - 1)).astype(F32)


def rows_of(count, columns):
    return lax.broadcasted_iota(jnp.int32, (count, columns), 0).astype(F32)


def ones_where(mask):
    return jnp.where(mask, jnp.ones((), BF), jnp.zeros((), BF))


def one_hot(lo):
    upper = jnp.where(lo >= 256, 1.0, 0.0)
    lower = (lo - 256 * upper).astype(BF)
    upper = upper.astype(BF)
    rows = rows_of(256, lo.shape[1]).astype(BF)
    none = jnp.array(-1, BF)
    return jnp.concatenate(
        [ones_where(jnp.where(upper == jnp.array(u, BF), lower, none) == rows) for u in range(2)], axis=0
    )


def masked(v, hi):
    zero = jnp.zeros((), BF)
    return [jnp.where(hi == jnp.array(h, BF), v, zero) for h in range(HI)]


def add_sums(values, hi, hot, out_refs):
    top, rest, unscale = split(values)
    members = ones_where(hi == rows_of(HI, hi.shape[1]).astype(BF))
    left = jnp.concatenate(masked(top, hi) + [members], axis=0)
    s = lax.dot_general(left, hot, NT, preferred_element_type=F32)
    left = jnp.concatenate(masked(rest.astype(BF), hi), axis=0).astype(F8)
    fine = lax.dot_general(left, hot.astype(F8), NT, preferred_element_type=F32)
    sums = s[: HI * F] + fine * unscale
    counts = s[HI * F :]
    for p, out_ref in enumerate(out_refs):
        columns = slice(p * WIDTH, (p + 1) * WIDTH)
        for y in range(Y):
            out_ref[y, :SUM_ROWS, :] += sums[y * SUM_ROWS : (y + 1) * SUM_ROWS, columns]
            out_ref[y, SUM_ROWS : SUM_ROWS + Z, :] += counts[y * Z : (y + 1) * Z, columns]


def looked_up(terms, hi, hot):
    g = jnp.dot(terms, jnp.concatenate([hot, hot], axis=0), preferred_element_type=F32)
    hi = hi.astype(F32)
    found = g[:F]
    for h in range(1, HI):
        found = jnp.where(hi == h, g[h * F : (h + 1) * F], found)
    return found


def terms_of(table_refs):
    v = jnp.concatenate([ref[...] for ref in table_refs], axis=1)
    top = v.astype(BF)
    return jnp.concatenate([top, (v - top.astype(F32)).astype(BF)], axis=1)


def chunks(body):
    for at in range(0, TILE, CHUNK):
        body(slice(at, at + CHUNK))


def squares_kernel(e_ref, out_ref):
    values = e_ref[...].astype(F32)
    total = jnp.sum(values * values, axis=0, keepdims=True)
    for at in range(out_ref.shape[0]):
        out_ref[at] = total


def first_kernel(with_init, values_ref, codes_ref, *refs):
    out_refs = refs[-PARTS:]

    @pl.when(pl.program_id(0) == 0)
    def _():
        for p, out_ref in enumerate(out_refs):
            out_ref[...] = refs[p][...] if with_init else jnp.zeros_like(out_ref)

    def body(at):
        hi, lo = hi_lo(codes_ref[0:1, at])
        add_sums(values_ref[:, at], hi, one_hot(lo), out_refs)

    chunks(body)


def second_kernel(tiles, mine_ref, my_codes_ref, theirs_ref, their_codes_ref, *refs):
    table_refs, middle_ref, out_refs = refs[:PARTS], refs[PARTS], refs[PARTS + 1 :]
    step = pl.program_id(0)
    terms = terms_of(table_refs)

    @pl.when(step == 0)
    def _():
        for out_ref in out_refs:
            out_ref[...] = jnp.zeros_like(out_ref)

    def body(at):
        values = jnp.where(step < tiles, mine_ref[:, at], theirs_ref[:, at])
        codes = jnp.where(step < tiles, my_codes_ref[0:2, at], their_codes_ref[0:2, at])
        hi, lo = hi_lo(codes[0:1])
        middle = values - looked_up(terms, hi, one_hot(lo))
        middle_ref[:, at] = middle
        hi, lo = hi_lo(codes[1:2])
        add_sums(middle, hi, one_hot(lo), out_refs)

    chunks(body)


def last_kernel(middle_ref, codes_ref, *refs):
    table_refs, tail_refs, out_ref = refs[:PARTS], refs[PARTS:-1], refs[-1]
    terms = terms_of(table_refs)

    def body(at):
        hi, lo = hi_lo(codes_ref[1:2, at])
        out_ref[:F, at] = middle_ref[:, at] - looked_up(terms, hi, one_hot(lo))

    chunks(body)
    for ref in tail_refs:
        out_ref[F:, :] = ref[...]


def whole(*shape):
    return pl.BlockSpec(shape, lambda *i: (0,) * len(shape))


def cost(products, columns):
    return pl.CostEstimate(flops=products * 4 * HI * F * LO * columns, bytes_accessed=8 * F * columns, transcendentals=0)


SUMS = [jax.ShapeDtypeStruct((Y, BLOCK, WIDTH), F32)] * PARTS
SUM_SPECS = [whole(Y, BLOCK, WIDTH)] * PARTS
TABLE_SPECS = [whole(HI * F, WIDTH)] * PARTS
PARAMS = pltpu.CompilerParams(vmem_limit_bytes=32 << 20)


def squares_of(e, copies):
    rows, n = e.shape
    return pl.pallas_call(
        squares_kernel,
        grid=(2,),
        in_specs=[pl.BlockSpec((rows, n // 2), lambda i: (0, i))],
        out_specs=pl.BlockSpec((copies, 1, n // 2), lambda i: (0, 0, i)),
        out_shape=jax.ShapeDtypeStruct((copies, 1, n), F32),
        compiler_params=PARAMS,
        name="squares",
    )(e)


def first_sums(packed, init=()):
    n = packed.shape[1]
    return pl.pallas_call(
        functools.partial(first_kernel, len(init) > 0),
        grid=(n // TILE,),
        in_specs=[pl.BlockSpec((F, TILE), lambda i: (0, i)), pl.BlockSpec((8, TILE), lambda i: (F // 8, i))]
        + SUM_SPECS[: len(init)],
        out_specs=SUM_SPECS,
        out_shape=SUMS,
        compiler_params=PARAMS,
        cost_estimate=cost(1, n),
        name="first_sums",
    )(packed, packed, *init)


def second_sums(mine, theirs, tables):
    n = mine.shape[1]
    tiles = n // TILE

    def early(i):
        return jnp.minimum(i, tiles - 1)

    def late(i):
        return jnp.maximum(i - tiles, 0)

    return pl.pallas_call(
        functools.partial(second_kernel, tiles),
        grid=(2 * tiles,),
        in_specs=[
            pl.BlockSpec((F, TILE), lambda i: (0, early(i))),
            pl.BlockSpec((8, TILE), lambda i: (F // 8, early(i))),
            pl.BlockSpec((F, TILE), lambda i: (0, late(i))),
            pl.BlockSpec((8, TILE), lambda i: (F // 8, late(i))),
            *TABLE_SPECS,
        ],
        out_specs=[pl.BlockSpec((F, TILE), lambda i: (0, i)), *SUM_SPECS],
        out_shape=[jax.ShapeDtypeStruct((F, 2 * n), F32), *SUMS],
        compiler_params=PARAMS,
        cost_estimate=cost(2, 2 * n),
        name="second_sums",
    )(mine, mine, theirs, theirs, *tables)


def last_lookup(middle, part, packed, tables, tail=()):
    n = packed.shape[1]
    rows = F + 8 * len(tail)
    tiles = n // TILE
    return pl.pallas_call(
        last_kernel,
        grid=(tiles,),
        in_specs=[
            pl.BlockSpec((F, TILE), lambda i: (0, part * tiles + i)),
            pl.BlockSpec((8, TILE), lambda i: (F // 8, i)),
            *TABLE_SPECS,
        ]
        + [pl.BlockSpec((8, TILE), lambda i: (0, i))] * len(tail),
        out_specs=pl.BlockSpec((rows, TILE), lambda i: (0, i)),
        out_shape=jax.ShapeDtypeStruct((rows, n), F32),
        compiler_params=PARAMS,
        cost_estimate=cost(1, n),
        name="last_lookup",
    )(middle, packed, *tables, *tail)


def to_all(v, axis, size=4):
    return lax.all_to_all(jnp.broadcast_to(v[None], (size, *v.shape)), axis, 0, 0, tiled=True)


def swap_core(v):
    return lax.ppermute(v, "core", [(0, 1), (1, 0)])


def swap_z(v, first):
    steps = (1, 3) if first else (3, 1)
    pairs = [(2 * z + c, 2 * (z ^ steps[c]) + c) for z in range(Z) for c in range(2)]
    return lax.ppermute(v, ("zh", "core"), pairs)


def at_y(parts):
    return [lax.all_to_all(part, "y", 0, 0, tiled=True).sum(axis=0) for part in parts]


def over_z(parts, first):
    return [part + swap_z(part, first) for part in parts]


def over_z_with(parts, old, core, zh):
    (own,) = parts
    got = swap_z(jnp.concatenate([own, old]), True)
    own, olds = own + got[:BLOCK], [old, got[BLOCK:]]
    got = swap_z(jnp.concatenate([own, *olds]), False)
    own, olds = own + got[:BLOCK], jnp.stack([*olds, got[BLOCK : BLOCK + F], got[BLOCK + F :]])
    near, far = jnp.where(core == 0, olds[1], olds[2]), jnp.where(core == 0, olds[2], olds[1])
    olds = jnp.stack([olds[0], near, olds[3], far])
    olds = jnp.where(zh % 2 == 0, olds, jnp.stack([olds[1], olds[0], olds[3], olds[2]]))
    olds = jnp.where(zh < 2, olds, jnp.concatenate([olds[2:], olds[:2]]))
    return [own], olds


def updated(parts, olds):
    news = []
    for p, own in enumerate(parts):
        counts = own[SUM_ROWS : SUM_ROWS + Z, None, :]
        old = olds[:, :, p * WIDTH : (p + 1) * WIDTH]
        news.append(0.5 * old + 0.5 * own[:SUM_ROWS].reshape(Z, F, WIDTH) / (counts + 1.0))
    return news


def tables_of(news):
    return [to_all(new, "y").reshape(HI * F, WIDTH) for new in news]


def on_device(e, first_codes, second_codes, first_old, second_old):
    core, zh = lax.axis_index("core"), lax.axis_index("zh")
    n = e.shape[1]

    def feature_half(v, which, axis):
        return lax.dynamic_slice_in_dim(v, which * F, F, axis)

    def by_core(mine, theirs, axis):
        return jnp.where(core == 0, jnp.concatenate([mine, theirs], axis), jnp.concatenate([theirs, mine], axis))

    def owned(news):
        own = lax.dynamic_index_in_dim(jnp.concatenate(news, axis=2), zh, keepdims=False)
        first, last = own[:, :256], own[:, 256:]
        return jnp.where(core == 0, first, last), jnp.where(core == 0, last, first)

    values = e.astype(F32)
    squares = lax.all_to_all(squares_of(e, 4), "x", 0, 0, tiled=True).reshape(4, n).sum(axis=0)
    squares = to_all(squares, "zl").sum(axis=0)
    normed = values * lax.rsqrt(squares / D + 1e-06)[None, :]
    codes = jnp.stack([first_codes, second_codes]).astype(F32)

    def packed(half):
        olds = jnp.stack([feature_half(first_old, half, 0), feature_half(second_old, half, 0)])
        return jnp.concatenate([feature_half(normed, half, 0), codes, olds.reshape(1, n), jnp.zeros((5, n), F32)])

    mine = packed(core)
    theirs = swap_core(packed(1 - core))

    sums = first_sums(theirs, first_sums(mine))
    olds = by_core(mine[F + 2].reshape(2, F, 256), theirs[F + 2].reshape(2, F, 256), 2)
    own, old = over_z_with(at_y(sums), olds[0], core, zh)
    first_news = updated(own, old)

    middle, *sums = second_sums(mine, theirs, tables_of(first_news))
    own, first_news = lax.optimization_barrier((at_y(sums), first_news))
    own, old = over_z_with(own, olds[1], core, zh)
    kept, sent = owned(first_news)
    own, first_new = lax.optimization_barrier((own, by_core(kept, swap_core(sent), 0)))
    second_news = updated(own, old)

    tables, second_news = lax.optimization_barrier((tables_of(second_news), second_news))
    kept, sent = owned(second_news)
    tail = jnp.concatenate([sent.reshape(1, -1), jnp.zeros((1, n - sent.size), F32)], axis=1)
    got = swap_core(last_lookup(middle, 1, theirs, tables, [jnp.broadcast_to(tail, (8, n))]))
    rest = last_lookup(middle, 0, mine, tables)
    second_new = by_core(kept, got[F, : sent.size].reshape(sent.shape), 0)
    return first_new, second_new, by_core(rest, got[:F], 0)


def solution(mesh):
    grid = Mesh(mesh.devices.reshape(Y, Z, 2, 4, 4), ("y", "zh", "core", "zl", "x"))
    item, code = ("y", "zh", "core"), ("zl", "x")
    both = P(code, item)
    return jax.shard_map(
        on_device,
        mesh=grid,
        in_specs=(both, P(item), P(item), both, both),
        out_specs=(both, both, both),
        check_vma=False,
    )
```

```python
import functools

import jax
import jax.numpy as jnp
from jax import lax
from jax.experimental import pallas as pl
from jax.experimental.pallas import tpu as pltpu
from jax.sharding import Mesh
from jax.sharding import PartitionSpec as P

D = 512
HI = 16
LO = 512
Y = 4
Z = 4
F = 16
SUM_ROWS = Z * F
BLOCK = SUM_ROWS + 8
TILE = 4096
CHUNK = 4096
BF = jnp.bfloat16
F8 = jnp.float8_e4m3fn
REST_MAX = 256.0
F32 = jnp.float32
NT = (((1,), (1,)), ((), ()))
PARTS = 1
WIDTH = LO // PARTS


def split(v):
    top = v.astype(BF)
    largest = jnp.maximum(jnp.max(jnp.abs(v), keepdims=True), 1e-30)
    scale = (REST_MAX * 256.0) / largest
    return top, (v - top.astype(F32)) * scale, largest * (1.0 / (REST_MAX * 256.0))


def hi_lo(code):
    code = code.astype(jnp.int32)
    return (code >> 9).astype(F32).astype(BF), (code & (LO - 1)).astype(F32)


def rows_of(count, columns):
    return lax.broadcasted_iota(jnp.int32, (count, columns), 0).astype(F32)


def ones_where(mask):
    return jnp.where(mask, jnp.ones((), BF), jnp.zeros((), BF))


def one_hot(lo):
    upper = jnp.where(lo >= 256, 1.0, 0.0)
    lower = (lo - 256 * upper).astype(BF)
    upper = upper.astype(BF)
    rows = rows_of(256, lo.shape[1]).astype(BF)
    none = jnp.array(-1, BF)
    return jnp.concatenate(
        [ones_where(jnp.where(upper == jnp.array(u, BF), lower, none) == rows) for u in range(2)], axis=0
    )


def masked(v, hi):
    zero = jnp.zeros((), BF)
    return [jnp.where(hi == jnp.array(h, BF), v, zero) for h in range(HI)]


def add_sums(values, hi, hot, out_refs):
    top, rest, unscale = split(values)
    members = ones_where(hi == rows_of(HI, hi.shape[1]).astype(BF))
    left = jnp.concatenate(masked(top, hi) + [members], axis=0)
    s = lax.dot_general(left, hot, NT, preferred_element_type=F32)
    left = jnp.concatenate(masked(rest.astype(BF), hi), axis=0).astype(F8)
    fine = lax.dot_general(left, hot.astype(F8), NT, preferred_element_type=F32)
    sums = s[: HI * F] + fine * unscale
    counts = s[HI * F :]
    for p, out_ref in enumerate(out_refs):
        columns = slice(p * WIDTH, (p + 1) * WIDTH)
        for y in range(Y):
            out_ref[y, :SUM_ROWS, :] += sums[y * SUM_ROWS : (y + 1) * SUM_ROWS, columns]
            out_ref[y, SUM_ROWS : SUM_ROWS + Z, :] += counts[y * Z : (y + 1) * Z, columns]


def looked_up(terms, hi, hot):
    g = jnp.dot(terms, jnp.concatenate([hot, hot], axis=0), preferred_element_type=F32)
    hi = hi.astype(F32)
    found = g[:F]
    for h in range(1, HI):
        found = jnp.where(hi == h, g[h * F : (h + 1) * F], found)
    return found


def terms_of(table_refs):
    v = jnp.concatenate([ref[...] for ref in table_refs], axis=1)
    top = v.astype(BF)
    return jnp.concatenate([top, (v - top.astype(F32)).astype(BF)], axis=1)


def chunks(body):
    for at in range(0, TILE, CHUNK):
        body(slice(at, at + CHUNK))


def squares_kernel(e_ref, out_ref):
    values = e_ref[...].astype(F32)
    total = jnp.sum(values * values, axis=0, keepdims=True)
    for at in range(out_ref.shape[0]):
        out_ref[at] = total


def first_kernel(with_init, values_ref, codes_ref, *refs):
    out_refs = refs[-PARTS:]

    @pl.when(pl.program_id(0) == 0)
    def _():
        for p, out_ref in enumerate(out_refs):
            out_ref[...] = refs[p][...] if with_init else jnp.zeros_like(out_ref)

    def body(at):
        hi, lo = hi_lo(codes_ref[0:1, at])
        add_sums(values_ref[:, at], hi, one_hot(lo), out_refs)

    chunks(body)


def second_kernel(tiles, mine_ref, my_codes_ref, theirs_ref, their_codes_ref, *refs):
    table_refs, middle_ref, out_refs = refs[:PARTS], refs[PARTS], refs[PARTS + 1 :]
    step = pl.program_id(0)
    terms = terms_of(table_refs)

    @pl.when(step == 0)
    def _():
        for out_ref in out_refs:
            out_ref[...] = jnp.zeros_like(out_ref)

    def body(at):
        values = jnp.where(step < tiles, mine_ref[:, at], theirs_ref[:, at])
        codes = jnp.where(step < tiles, my_codes_ref[0:2, at], their_codes_ref[0:2, at])
        hi, lo = hi_lo(codes[0:1])
        middle = values - looked_up(terms, hi, one_hot(lo))
        middle_ref[:, at] = middle
        hi, lo = hi_lo(codes[1:2])
        add_sums(middle, hi, one_hot(lo), out_refs)

    chunks(body)


def last_kernel(middle_ref, codes_ref, *refs):
    table_refs, tail_refs, out_ref = refs[:PARTS], refs[PARTS:-1], refs[-1]
    terms = terms_of(table_refs)

    def body(at):
        hi, lo = hi_lo(codes_ref[1:2, at])
        out_ref[:F, at] = middle_ref[:, at] - looked_up(terms, hi, one_hot(lo))

    chunks(body)
    for ref in tail_refs:
        out_ref[F:, :] = ref[...]


def whole(*shape):
    return pl.BlockSpec(shape, lambda *i: (0,) * len(shape))


def cost(products, columns):
    return pl.CostEstimate(flops=products * 4 * HI * F * LO * columns, bytes_accessed=8 * F * columns, transcendentals=0)


SUMS = [jax.ShapeDtypeStruct((Y, BLOCK, WIDTH), F32)] * PARTS
SUM_SPECS = [whole(Y, BLOCK, WIDTH)] * PARTS
TABLE_SPECS = [whole(HI * F, WIDTH)] * PARTS
PARAMS = pltpu.CompilerParams(vmem_limit_bytes=32 << 20)


def squares_of(e, copies):
    rows, n = e.shape
    return pl.pallas_call(
        squares_kernel,
        grid=(2,),
        in_specs=[pl.BlockSpec((rows, n // 2), lambda i: (0, i))],
        out_specs=pl.BlockSpec((copies, 1, n // 2), lambda i: (0, 0, i)),
        out_shape=jax.ShapeDtypeStruct((copies, 1, n), F32),
        compiler_params=PARAMS,
        name="squares",
    )(e)


def first_sums(packed, init=()):
    n = packed.shape[1]
    return pl.pallas_call(
        functools.partial(first_kernel, len(init) > 0),
        grid=(n // TILE,),
        in_specs=[pl.BlockSpec((F, TILE), lambda i: (0, i)), pl.BlockSpec((8, TILE), lambda i: (F // 8, i))]
        + SUM_SPECS[: len(init)],
        out_specs=SUM_SPECS,
        out_shape=SUMS,
        compiler_params=PARAMS,
        cost_estimate=cost(1, n),
        name="first_sums",
    )(packed, packed, *init)


def second_sums(mine, theirs, tables):
    n = mine.shape[1]
    tiles = n // TILE

    def early(i):
        return jnp.minimum(i, tiles - 1)

    def late(i):
        return jnp.maximum(i - tiles, 0)

    return pl.pallas_call(
        functools.partial(second_kernel, tiles),
        grid=(2 * tiles,),
        in_specs=[
            pl.BlockSpec((F, TILE), lambda i: (0, early(i))),
            pl.BlockSpec((8, TILE), lambda i: (F // 8, early(i))),
            pl.BlockSpec((F, TILE), lambda i: (0, late(i))),
            pl.BlockSpec((8, TILE), lambda i: (F // 8, late(i))),
            *TABLE_SPECS,
        ],
        out_specs=[pl.BlockSpec((F, TILE), lambda i: (0, i)), *SUM_SPECS],
        out_shape=[jax.ShapeDtypeStruct((F, 2 * n), F32), *SUMS],
        compiler_params=PARAMS,
        cost_estimate=cost(2, 2 * n),
        name="second_sums",
    )(mine, mine, theirs, theirs, *tables)


def last_lookup(middle, part, packed, tables, tail=()):
    n = packed.shape[1]
    rows = F + 8 * len(tail)
    tiles = n // TILE
    return pl.pallas_call(
        last_kernel,
        grid=(tiles,),
        in_specs=[
            pl.BlockSpec((F, TILE), lambda i: (0, part * tiles + i)),
            pl.BlockSpec((8, TILE), lambda i: (F // 8, i)),
            *TABLE_SPECS,
        ]
        + [pl.BlockSpec((8, TILE), lambda i: (0, i))] * len(tail),
        out_specs=pl.BlockSpec((rows, TILE), lambda i: (0, i)),
        out_shape=jax.ShapeDtypeStruct((rows, n), F32),
        compiler_params=PARAMS,
        cost_estimate=cost(1, n),
        name="last_lookup",
    )(middle, packed, *tables, *tail)


def to_all(v, axis, size=4):
    return lax.all_to_all(jnp.broadcast_to(v[None], (size, *v.shape)), axis, 0, 0, tiled=True)


def swap_core(v):
    return lax.ppermute(v, "core", [(0, 1), (1, 0)])


def swap_z(v, step):
    steps = ((1, 3), (3, 1))[step]
    pairs = [(2 * z + c, 2 * (z ^ steps[c]) + c) for z in range(Z) for c in range(2)]
    return lax.ppermute(v, ("zh", "core"), pairs)


def at_y(parts):
    return [lax.all_to_all(part, "y", 0, 0, tiled=True).sum(axis=0) for part in parts]


def over_z_with(parts, old, core, zh, order):
    (own,) = parts
    got = swap_z(jnp.concatenate([own, old]), order[0])
    own, olds = own + got[:BLOCK], [old, got[BLOCK:]]
    got = swap_z(jnp.concatenate([own, *olds]), order[1])
    own, olds = own + got[:BLOCK], [*olds, got[BLOCK : BLOCK + F], got[BLOCK + F :]]
    near_first = core == order[0]
    near, far = jnp.where(near_first, olds[1], olds[2]), jnp.where(near_first, olds[2], olds[1])
    olds = jnp.stack([olds[0], near, olds[3], far])
    olds = jnp.where(zh % 2 == 0, olds, jnp.stack([olds[1], olds[0], olds[3], olds[2]]))
    olds = jnp.where(zh < 2, olds, jnp.concatenate([olds[2:], olds[:2]]))
    return [own], olds


def updated(parts, olds):
    news = []
    for p, own in enumerate(parts):
        counts = own[SUM_ROWS : SUM_ROWS + Z, None, :]
        old = olds[:, :, p * WIDTH : (p + 1) * WIDTH]
        news.append(0.5 * old + 0.5 * own[:SUM_ROWS].reshape(Z, F, WIDTH) / (counts + 1.0))
    return news


def tables_of(news):
    return [to_all(new, "y").reshape(HI * F, WIDTH) for new in news]


def on_device(e, first_codes, second_codes, first_old, second_old):
    core, zh = lax.axis_index("core"), lax.axis_index("zh")
    n = e.shape[1]

    def feature_half(v, which, axis):
        return lax.dynamic_slice_in_dim(v, which * F, F, axis)

    def by_core(mine, theirs, axis):
        return jnp.where(core == 0, jnp.concatenate([mine, theirs], axis), jnp.concatenate([theirs, mine], axis))

    def owned(news):
        own = lax.dynamic_index_in_dim(jnp.concatenate(news, axis=2), zh, keepdims=False)
        first, last = own[:, :256], own[:, 256:]
        return jnp.where(core == 0, first, last), jnp.where(core == 0, last, first)

    values = e.astype(F32)
    squares = lax.all_to_all(squares_of(e, 4), "x", 0, 0, tiled=True).reshape(4, n).sum(axis=0)
    squares = to_all(squares, "zl").sum(axis=0)
    normed = values * lax.rsqrt(squares / D + 1e-06)[None, :]
    codes = jnp.stack([first_codes, second_codes]).astype(F32)

    def packed(half):
        olds = jnp.stack([feature_half(first_old, half, 0), feature_half(second_old, half, 0)])
        return jnp.concatenate([feature_half(normed, half, 0), codes, olds.reshape(1, n), jnp.zeros((5, n), F32)])

    mine = packed(core)
    theirs = swap_core(packed(1 - core))

    sums = first_sums(theirs, first_sums(mine))
    olds = by_core(mine[F + 2].reshape(2, F, 256), theirs[F + 2].reshape(2, F, 256), 2)
    own, old = over_z_with(at_y(sums), olds[0], core, zh, (0, 1))
    first_news = updated(own, old)

    middle, *sums = second_sums(mine, theirs, tables_of(first_news))
    own, first_news = lax.optimization_barrier((at_y(sums), first_news))
    own, old = over_z_with(own, olds[1], core, zh, (1, 0))
    kept, sent = owned(first_news)
    own, first_new = lax.optimization_barrier((own, by_core(kept, swap_core(sent), 0)))
    second_news = updated(own, old)

    tables, second_news = lax.optimization_barrier((tables_of(second_news), second_news))
    kept, sent = owned(second_news)
    tail = jnp.concatenate([sent.reshape(1, -1), jnp.zeros((1, n - sent.size), F32)], axis=1)
    got = swap_core(last_lookup(middle, 1, theirs, tables, [jnp.broadcast_to(tail, (8, n))]))
    rest = last_lookup(middle, 0, mine, tables)
    second_new = by_core(kept, got[F, : sent.size].reshape(sent.shape), 0)
    return first_new, second_new, by_core(rest, got[:F], 0)


def solution(mesh):
    grid = Mesh(mesh.devices.reshape(Y, Z, 2, 4, 4), ("y", "zh", "core", "zl", "x"))
    item, code = ("y", "zh", "core"), ("zl", "x")
    both = P(code, item)
    return jax.shard_map(
        on_device,
        mesh=grid,
        in_specs=(both, P(item), P(item), both, both),
        out_specs=(both, both, both),
        check_vma=False,
    )
```

```python
import functools

import jax
import jax.numpy as jnp
from jax import lax
from jax.experimental import pallas as pl
from jax.experimental.pallas import tpu as pltpu
from jax.sharding import Mesh
from jax.sharding import PartitionSpec as P

D = 512
HI = 16
LO = 512
Y = 4
Z = 4
F = 16
SUM_ROWS = Z * F
BLOCK = SUM_ROWS + 8
TILE = 4096
CHUNK = 4096
BF = jnp.bfloat16
F8 = jnp.float8_e4m3fn
REST_MAX = 256.0
F32 = jnp.float32
NT = (((1,), (1,)), ((), ()))
PARTS = 1
WIDTH = LO // PARTS


def split(v):
    top = v.astype(BF)
    largest = jnp.maximum(jnp.max(jnp.abs(v), keepdims=True), 1e-30)
    scale = (REST_MAX * 256.0) / largest
    return top, (v - top.astype(F32)) * scale, largest * (1.0 / (REST_MAX * 256.0))


def hi_lo(code):
    code = code.astype(jnp.int32)
    return (code >> 9).astype(F32).astype(BF), (code & (LO - 1)).astype(F32)


def rows_of(count, columns):
    return lax.broadcasted_iota(jnp.int32, (count, columns), 0).astype(F32)


def ones_where(mask):
    return jnp.where(mask, jnp.ones((), BF), jnp.zeros((), BF))


def one_hot(lo):
    upper = jnp.where(lo >= 256, 1.0, 0.0)
    lower = (lo - 256 * upper).astype(BF)
    upper = upper.astype(BF)
    rows = rows_of(256, lo.shape[1]).astype(BF)
    none = jnp.array(-1, BF)
    return jnp.concatenate(
        [ones_where(jnp.where(upper == jnp.array(u, BF), lower, none) == rows) for u in range(2)], axis=0
    )


def masked(v, hi):
    zero = jnp.zeros((), BF)
    return [jnp.where(hi == jnp.array(h, BF), v, zero) for h in range(HI)]


def add_sums(values, hi, hot, out_refs):
    top, rest, unscale = split(values)
    members = ones_where(hi == rows_of(HI, hi.shape[1]).astype(BF))
    left = jnp.concatenate(masked(top, hi) + [members], axis=0)
    s = lax.dot_general(left, hot, NT, preferred_element_type=F32)
    left = jnp.concatenate(masked(rest.astype(BF), hi), axis=0).astype(F8)
    fine = lax.dot_general(left, hot.astype(F8), NT, preferred_element_type=F32)
    sums = s[: HI * F] + fine * unscale
    counts = s[HI * F :]
    for p, out_ref in enumerate(out_refs):
        columns = slice(p * WIDTH, (p + 1) * WIDTH)
        for y in range(Y):
            out_ref[y, :SUM_ROWS, :] += sums[y * SUM_ROWS : (y + 1) * SUM_ROWS, columns]
            out_ref[y, SUM_ROWS : SUM_ROWS + Z, :] += counts[y * Z : (y + 1) * Z, columns]


def looked_up(terms, hi, hot):
    g = jnp.dot(terms, jnp.concatenate([hot, hot], axis=0), preferred_element_type=F32)
    hi = hi.astype(F32)
    found = g[:F]
    for h in range(1, HI):
        found = jnp.where(hi == h, g[h * F : (h + 1) * F], found)
    return found


def terms_of(table_refs):
    v = jnp.concatenate([ref[...] for ref in table_refs], axis=1)
    top = v.astype(BF)
    return jnp.concatenate([top, (v - top.astype(F32)).astype(BF)], axis=1)


def chunks(body):
    for at in range(0, TILE, CHUNK):
        body(slice(at, at + CHUNK))


def squares_kernel(e_ref, out_ref):
    values = e_ref[...].astype(F32)
    total = jnp.sum(values * values, axis=0, keepdims=True)
    for at in range(out_ref.shape[0]):
        out_ref[at] = total


def first_kernel(with_init, values_ref, codes_ref, *refs):
    out_refs = refs[-PARTS:]

    @pl.when(pl.program_id(0) == 0)
    def _():
        for p, out_ref in enumerate(out_refs):
            out_ref[...] = refs[p][...] if with_init else jnp.zeros_like(out_ref)

    def body(at):
        hi, lo = hi_lo(codes_ref[0:1, at])
        add_sums(values_ref[:, at], hi, one_hot(lo), out_refs)

    chunks(body)


def second_kernel(tiles, mine_ref, my_codes_ref, theirs_ref, their_codes_ref, *refs):
    table_refs, middle_ref, out_refs = refs[:PARTS], refs[PARTS], refs[PARTS + 1 :]
    step = pl.program_id(0)
    terms = terms_of(table_refs)

    @pl.when(step == 0)
    def _():
        for out_ref in out_refs:
            out_ref[...] = jnp.zeros_like(out_ref)

    def body(at):
        values = jnp.where(step < tiles, mine_ref[:, at], theirs_ref[:, at])
        codes = jnp.where(step < tiles, my_codes_ref[0:2, at], their_codes_ref[0:2, at])
        hi, lo = hi_lo(codes[0:1])
        middle = values - looked_up(terms, hi, one_hot(lo))
        middle_ref[:, at] = middle
        hi, lo = hi_lo(codes[1:2])
        add_sums(middle, hi, one_hot(lo), out_refs)

    chunks(body)


def last_kernel(middle_ref, codes_ref, *refs):
    table_refs, tail_refs, out_ref = refs[:PARTS], refs[PARTS:-1], refs[-1]
    terms = terms_of(table_refs)

    def body(at):
        hi, lo = hi_lo(codes_ref[1:2, at])
        out_ref[:F, at] = middle_ref[:, at] - looked_up(terms, hi, one_hot(lo))

    chunks(body)
    for ref in tail_refs:
        out_ref[F:, :] = ref[...]


def whole(*shape):
    return pl.BlockSpec(shape, lambda *i: (0,) * len(shape))


def cost(products, columns):
    return pl.CostEstimate(flops=products * 4 * HI * F * LO * columns, bytes_accessed=8 * F * columns, transcendentals=0)


SUMS = [jax.ShapeDtypeStruct((Y, BLOCK, WIDTH), F32)] * PARTS
SUM_SPECS = [whole(Y, BLOCK, WIDTH)] * PARTS
TABLE_SPECS = [whole(HI * F, WIDTH)] * PARTS
PARAMS = pltpu.CompilerParams(vmem_limit_bytes=32 << 20)


def squares_of(e, copies):
    rows, n = e.shape
    return pl.pallas_call(
        squares_kernel,
        grid=(2,),
        in_specs=[pl.BlockSpec((rows, n // 2), lambda i: (0, i))],
        out_specs=pl.BlockSpec((copies, 1, n // 2), lambda i: (0, 0, i)),
        out_shape=jax.ShapeDtypeStruct((copies, 1, n), F32),
        compiler_params=PARAMS,
        name="squares",
    )(e)


def first_sums(packed, init=()):
    n = packed.shape[1]
    return pl.pallas_call(
        functools.partial(first_kernel, len(init) > 0),
        grid=(n // TILE,),
        in_specs=[pl.BlockSpec((F, TILE), lambda i: (0, i)), pl.BlockSpec((8, TILE), lambda i: (F // 8, i))]
        + SUM_SPECS[: len(init)],
        out_specs=SUM_SPECS,
        out_shape=SUMS,
        compiler_params=PARAMS,
        cost_estimate=cost(1, n),
        name="first_sums",
    )(packed, packed, *init)


def second_sums(mine, theirs, tables):
    n = mine.shape[1]
    tiles = n // TILE

    def early(i):
        return jnp.minimum(i, tiles - 1)

    def late(i):
        return jnp.maximum(i - tiles, 0)

    return pl.pallas_call(
        functools.partial(second_kernel, tiles),
        grid=(2 * tiles,),
        in_specs=[
            pl.BlockSpec((F, TILE), lambda i: (0, early(i))),
            pl.BlockSpec((8, TILE), lambda i: (F // 8, early(i))),
            pl.BlockSpec((F, TILE), lambda i: (0, late(i))),
            pl.BlockSpec((8, TILE), lambda i: (F // 8, late(i))),
            *TABLE_SPECS,
        ],
        out_specs=[pl.BlockSpec((F, TILE), lambda i: (0, i)), *SUM_SPECS],
        out_shape=[jax.ShapeDtypeStruct((F, 2 * n), F32), *SUMS],
        compiler_params=PARAMS,
        cost_estimate=cost(2, 2 * n),
        name="second_sums",
    )(mine, mine, theirs, theirs, *tables)


def last_lookup(middle, part, packed, tables, tail=()):
    n = packed.shape[1]
    rows = F + 8 * len(tail)
    tiles = n // TILE
    return pl.pallas_call(
        last_kernel,
        grid=(tiles,),
        in_specs=[
            pl.BlockSpec((F, TILE), lambda i: (0, part * tiles + i)),
            pl.BlockSpec((8, TILE), lambda i: (F // 8, i)),
            *TABLE_SPECS,
        ]
        + [pl.BlockSpec((8, TILE), lambda i: (0, i))] * len(tail),
        out_specs=pl.BlockSpec((rows, TILE), lambda i: (0, i)),
        out_shape=jax.ShapeDtypeStruct((rows, n), F32),
        compiler_params=PARAMS,
        cost_estimate=cost(1, n),
        name="last_lookup",
    )(middle, packed, *tables, *tail)


def to_all(v, axis, size=4):
    return lax.all_to_all(jnp.broadcast_to(v[None], (size, *v.shape)), axis, 0, 0, tiled=True)


def swap_core(v):
    return lax.ppermute(v, "core", [(0, 1), (1, 0)])


def swap_z(v, step):
    steps = ((1, 3), (3, 1))[step]
    pairs = [(2 * z + c, 2 * (z ^ steps[c]) + c) for z in range(Z) for c in range(2)]
    return lax.ppermute(v, ("zh", "core"), pairs)


def at_y(parts):
    return [lax.all_to_all(part, "y", 0, 0, tiled=True).sum(axis=0) for part in parts]


def over_z_with(parts, old, core, zh, order, beside=()):
    (own,) = parts
    got = swap_z(jnp.concatenate([own, old]), order[0])
    got, beside = lax.optimization_barrier((got, beside))
    own, olds = own + got[:BLOCK], [old, got[BLOCK:]]
    got = swap_z(jnp.concatenate([own, *olds]), order[1])
    own, olds = own + got[:BLOCK], [*olds, got[BLOCK : BLOCK + F], got[BLOCK + F :]]
    near_first = core == order[0]
    near, far = jnp.where(near_first, olds[1], olds[2]), jnp.where(near_first, olds[2], olds[1])
    olds = jnp.stack([olds[0], near, olds[3], far])
    olds = jnp.where(zh % 2 == 0, olds, jnp.stack([olds[1], olds[0], olds[3], olds[2]]))
    olds = jnp.where(zh < 2, olds, jnp.concatenate([olds[2:], olds[:2]]))
    return [own], olds, beside


def updated(parts, olds):
    news = []
    for p, own in enumerate(parts):
        counts = own[SUM_ROWS : SUM_ROWS + Z, None, :]
        old = olds[:, :, p * WIDTH : (p + 1) * WIDTH]
        news.append(0.5 * old + 0.5 * own[:SUM_ROWS].reshape(Z, F, WIDTH) / (counts + 1.0))
    return news


def tables_of(news):
    return [to_all(new, "y").reshape(HI * F, WIDTH) for new in news]


def on_device(e, first_codes, second_codes, first_old, second_old):
    core, zh = lax.axis_index("core"), lax.axis_index("zh")
    n = e.shape[1]

    def feature_half(v, which, axis):
        return lax.dynamic_slice_in_dim(v, which * F, F, axis)

    def by_core(mine, theirs, axis):
        return jnp.where(core == 0, jnp.concatenate([mine, theirs], axis), jnp.concatenate([theirs, mine], axis))

    def owned(news):
        own = lax.dynamic_index_in_dim(jnp.concatenate(news, axis=2), zh, keepdims=False)
        first, last = own[:, :256], own[:, 256:]
        return jnp.where(core == 0, first, last), jnp.where(core == 0, last, first)

    values = e.astype(F32)
    squares = lax.all_to_all(squares_of(e, 4), "x", 0, 0, tiled=True).reshape(4, n).sum(axis=0)
    squares = to_all(squares, "zl").sum(axis=0)
    normed = values * lax.rsqrt(squares / D + 1e-06)[None, :]
    codes = jnp.stack([first_codes, second_codes]).astype(F32)

    def packed(half):
        olds = jnp.stack([feature_half(first_old, half, 0), feature_half(second_old, half, 0)])
        return jnp.concatenate([feature_half(normed, half, 0), codes, olds.reshape(1, n), jnp.zeros((5, n), F32)])

    mine = packed(core)
    theirs = swap_core(packed(1 - core))

    sums = first_sums(theirs, first_sums(mine))
    olds = by_core(mine[F + 2].reshape(2, F, 256), theirs[F + 2].reshape(2, F, 256), 2)
    own, old, _ = over_z_with(at_y(sums), olds[0], core, zh, (0, 1))
    first_news = updated(own, old)

    middle, *sums = second_sums(mine, theirs, tables_of(first_news))
    own, first_news = lax.optimization_barrier((at_y(sums), first_news))
    kept, sent = owned(first_news)
    first_new = by_core(kept, swap_core(sent), 0)
    own, old, first_new = over_z_with(own, olds[1], core, zh, (1, 0), first_new)
    second_news = updated(own, old)

    tables, second_news = lax.optimization_barrier((tables_of(second_news), second_news))
    kept, sent = owned(second_news)
    tail = jnp.concatenate([sent.reshape(1, -1), jnp.zeros((1, n - sent.size), F32)], axis=1)
    got = swap_core(last_lookup(middle, 1, theirs, tables, [jnp.broadcast_to(tail, (8, n))]))
    rest = last_lookup(middle, 0, mine, tables)
    second_new = by_core(kept, got[F, : sent.size].reshape(sent.shape), 0)
    return first_new, second_new, by_core(rest, got[:F], 0)


def solution(mesh):
    grid = Mesh(mesh.devices.reshape(Y, Z, 2, 4, 4), ("y", "zh", "core", "zl", "x"))
    item, code = ("y", "zh", "core"), ("zl", "x")
    both = P(code, item)
    return jax.shard_map(
        on_device,
        mesh=grid,
        in_specs=(both, P(item), P(item), both, both),
        out_specs=(both, both, both),
        check_vma=False,
    )
```
